256 devices in a mesh: expert: 32 (over x, z), dp: 8 (over y, core).
Axes of the slice: x: 4, y: 4, z: 8, core: 2. Of those that a mesh axis runs over, the one named last changes fastest.
Arguments:
- tokens: bfloat16 [8192, 2048], P('expert'), may hold values from -6 to 6
- cotangent: bfloat16 [8192, 2048], P('expert'), may hold values from -6 to 6
- expert_route: int32 [8192, 1], P('expert'), may hold values from 0 to 31; in each aligned block of 256 rows (0 to 255, 256 to 511, ...) at most 16 rows name the same one
- w_gate: bfloat16 [32, 2048, 7168], P('expert', None, 'dp'), may hold values from -0.125 to 0.125
- w_up: bfloat16 [32, 2048, 7168], P('expert', None, 'dp'), may hold values from -0.125 to 0.125
- w_down: bfloat16 [32, 7168, 2048], P('expert', 'dp'), may hold values from -0.0625 to 0.0625
- sign_seeds: int32 [32], P('expert'), may hold values from 0 to 65535
Outputs:
- tangent_grad: bfloat16 [8192, 2048], P('expert')
- curvature: float32 [32, 7168], P('expert', 'dp')
The draws below stay inside these ranges and needn't reach their ends.
Inputs may be any that keep to these rules, and one draw needn't show every extreme that they name: `expert_route`: among the tokens of one index of expert no expert is named more than 16 times, and in some index one expert is named exactly 16 times; every expert is named by some token.
All inputs are finite; a program needn't handle non-finite values.
Results may differ from the reference program's by a relative error of at most 0.005.
Values may be sent and summed in bfloat16 or wider, within the bound.
No kernel may reach another device: no remote copies, remote signals or barrier semaphores. Data moves between devices by JAX's collectives and lax.ppermute only.
A program may use at most 64 MiB of HBM per device.

```python
import math
import jax
import jax.numpy as jnp
import numpy as np
from jax import lax

D = 2048
FF = 7168
TOK_DEV = 256
EXPERTS = 32
CAP = 16
TOKENS = 8192
N_EXPERT = 32


def set_ends(result, stream_key, smallest, largest):
    shape = result.shape
    spot = [jax.random.randint(jax.random.fold_in(stream_key, axis), (), 0, shape[axis]) for axis in range(len(shape))]
    result = result.at[tuple(spot)].set(smallest)
    longest = shape.index(max(shape))
    spot[longest] = (spot[longest] + 1) % shape[longest]
    return result.at[tuple(spot)].set(largest)


def levels(rng, dims, split, least, largest):
    def one(dim, blocks):
        draws = jax.random.uniform(jax.random.fold_in(jax.random.fold_in(rng, 6), dim), (blocks,), jnp.float32, least / len(split), largest / len(split))
        return jnp.repeat(jnp.exp(draws), dims[dim] // blocks).reshape((-1,) + (1,) * (len(dims) - dim - 1))

    level = one(*split[0])
    for cut in split[1:]:
        level = level * one(*cut)
    return level


def assign_block(rng, own, number, rows, count, top, most, slope):
    ranking = jax.random.permutation(rng, count)
    heavy_load, ordinary = shares(count, rows * top, most, slope, True), shares(count, rows * top, most, slope, False)
    places = jnp.arange(count)

    def named(sizes, rotation):
        used = int((sizes > 0).sum())
        fixed = max(1, used // 4)
        passed = fixed + (places - fixed + rotation * (used - fixed)) % max(1, count - fixed)
        return jnp.zeros((count,), jnp.int32).at[ranking[jnp.where(places < fixed, places, passed)]].set(jnp.asarray(sizes, jnp.int32))

    sizes = jnp.where(number % 4 == 0, named(heavy_load, number // 4), named(ordinary, number - number // 4 - 1))
    mixed = jax.random.permutation(jax.random.fold_in(own, 3), count)
    source_of, sink = mixed[0:count // 2 * 2:2], mixed[1:count // 2 * 2:2]
    room = jnp.minimum(sizes[source_of] - 1, most - sizes[sink]) // 2
    room = jnp.where((source_of == ranking[0]) | (sink == ranking[0]) | (sizes[sink] == 0), 0, jnp.maximum(room, 0))
    passed = jax.random.randint(jax.random.fold_in(own, 4), (count // 2,), 0, 1 << 20) % (room + 1)
    sizes = sizes.at[source_of].add(-passed).at[sink].add(passed)
    labels = jnp.searchsorted(jnp.cumsum(sizes), jnp.arange(rows * top), side="right").astype(jnp.int32)
    listing = labels.reshape(top, rows).T
    listing = listing[jax.random.permutation(jax.random.fold_in(own, 1), rows)]
    rotation = jax.random.randint(jax.random.fold_in(own, 2), (rows, 1), 0, top)
    return jnp.take_along_axis(listing, (jnp.arange(top)[None, :] + rotation) % top, axis=1)


def shares(count, total, reach, lean, full):
    loads = [(1 << 20) // math.isqrt(standing ** lean) + 1 for standing in range(1, count + 1)]
    largest = reach if full else min(reach, max(-(-total // count), total * loads[0] // sum(loads)))
    least = 1 if total - largest >= count - 1 else 0
    given, rest = [largest] + [least] * (count - 1), total - largest - least * (count - 1)
    while rest > 0:
        free = [i for i in range(1, count) if given[i] < largest] or [i for i in range(1, count) if given[i] < reach]
        whole, budget = sum([loads[i] for i in free]), rest
        for i in free:
            more = min(reach - given[i], max(1, budget * loads[i] // whole), rest)
            given[i] = given[i] + more
            rest = rest - more
    return np.array(given)


def centred(own_key, dims, width, bound, split=(), kind=jnp.bfloat16):
    values = jax.random.normal(own_key, dims, jnp.float32) * width
    if len(split) > 0:
        values = levels(own_key, dims, split, -0.22, 0.18) * values
    return jnp.clip(values, min=-bound, max=bound).astype(kind)


def setup_inputs(seed: int = 0) -> dict:
    arg_keys = jax.random.split(jax.random.key(seed), 8)
    tokens = centred(arg_keys[0], (TOKENS, D), 1.0, 6.0, ((0, 32),))
    cotangent = centred(arg_keys[1], (TOKENS, D), 1.0, 6.0, ((0, 32),))
    expert_route_keys = jax.random.split(jax.random.fold_in(arg_keys[2], 1), TOKENS // TOK_DEV)
    expert_route_turns = jax.random.permutation(jax.random.fold_in(arg_keys[2], 3), TOKENS // TOK_DEV)
    expert_route = jax.vmap(lambda own, number: assign_block(jax.random.fold_in(arg_keys[2], 2), own, number, TOK_DEV, EXPERTS, 1, CAP, 2))(expert_route_keys, expert_route_turns).reshape((TOKENS, 1))
    w_gate = centred(arg_keys[3], (EXPERTS, D, FF), D ** -0.5, 0.125, ((0, 32), (2, 8)))
    w_up = centred(arg_keys[4], (EXPERTS, D, FF), D ** -0.5, 0.125, ((0, 32), (2, 8)))
    w_down = centred(arg_keys[5], (EXPERTS, FF, D), FF ** -0.5, 0.0625, ((0, 32), (1, 8)))
    sign_seeds = set_ends(jax.random.randint(arg_keys[6], (EXPERTS,), 0, 65536), jax.random.fold_in(arg_keys[6], 1), 0, 65535).astype(jnp.int32)
    return dict(tokens=tokens, cotangent=cotangent, expert_route=expert_route, w_gate=w_gate, w_up=w_up, w_down=w_down, sign_seeds=sign_seeds)


def mix_bits(row_index, col_index, seed_value):
    mixed = row_index * jnp.int32(73856093) + col_index * jnp.int32(19349663) + seed_value * jnp.int32(83492791)
    mixed = mixed ^ mixed >> 15
    mixed = mixed * jnp.int32(735632791)
    mixed = mixed ^ mixed >> 13
    mixed = mixed * jnp.int32(1274126177)
    mixed = mixed ^ mixed >> 16
    return mixed >> 5 & 1

def sign_table(row_index, col_index, seed_value, model_width):
    bits = mix_bits(row_index, col_index, seed_value)
    scale = jnp.asarray(1.0 / math.sqrt(model_width), jnp.bfloat16)
    return jnp.where(bits == 1, scale, -scale)

def silu_slopes(pre_act):
    sigmoid_pre = jax.nn.sigmoid(pre_act)
    slope_one = sigmoid_pre * (1.0 + pre_act * (1.0 - sigmoid_pre))
    slope_two = sigmoid_pre * (1.0 - sigmoid_pre) * (2.0 + pre_act * (1.0 - 2.0 * sigmoid_pre))
    return (slope_one, slope_two)

def expert_rows(rows_x, rows_cot, gate_mat, up_mat, down_mat, sign_values):
    contract = (((1,), (1,)), ((), ()))
    gate_pre = jnp.dot(rows_x, gate_mat, preferred_element_type=jnp.float32)
    up_pre = jnp.dot(rows_x, up_mat, preferred_element_type=jnp.float32)
    gate_tangent = jnp.dot(rows_x, sign_values, preferred_element_type=jnp.float32)
    hidden_grad = lax.dot_general(rows_cot, down_mat, contract, preferred_element_type=jnp.float32)
    slope_one, slope_two = silu_slopes(gate_pre)
    grad_gate = (hidden_grad * up_pre * slope_one).astype(jnp.bfloat16)
    tangent_gate = hidden_grad * up_pre * slope_two * gate_tangent
    tangent_up = (hidden_grad * slope_one * gate_tangent).astype(jnp.bfloat16)
    curvature = lax.optimization_barrier(jnp.sum(gate_tangent * tangent_gate, axis=0))
    tangent_grads = lax.dot_general(tangent_gate.astype(jnp.bfloat16), gate_mat, contract, preferred_element_type=jnp.float32)
    tangent_grads = tangent_grads + lax.dot_general(tangent_up, up_mat, contract, preferred_element_type=jnp.float32)
    tangent_grads = tangent_grads + lax.dot_general(grad_gate, sign_values, contract, preferred_element_type=jnp.float32)
    return (tangent_grads, curvature)

def reference(tokens, cotangent, expert_route, w_gate, w_up, w_down, sign_seeds):
    route_flat = expert_route[:, 0].astype(jnp.int32)
    expert_ids = jnp.arange(EXPERTS, dtype=jnp.int32)
    counts = lax.optimization_barrier(jnp.sum((route_flat[:, None] == expert_ids[None, :]).astype(jnp.int32), axis=0))
    starts = (jnp.cumsum(counts) - counts).astype(jnp.int32)
    most_rows = CAP * N_EXPERT
    sorted_tokens = jnp.argsort(route_flat, stable=True).astype(jnp.int32)
    padded_tokens = jnp.concatenate([sorted_tokens, jnp.zeros((most_rows,), jnp.int32)])
    row_index = jnp.arange(D, dtype=jnp.int32)[:, None]
    col_index = jnp.arange(FF, dtype=jnp.int32)[None, :]

    def one_expert(accumulated, expert_index):
        picked = lax.dynamic_slice_in_dim(padded_tokens, starts[expert_index].astype(jnp.int32), most_rows)
        live_rows = jnp.arange(most_rows, dtype=jnp.int32) < counts[expert_index]
        rows_x = jnp.where(live_rows[:, None], tokens[picked], jnp.zeros((), tokens.dtype))
        rows_cot = jnp.where(live_rows[:, None], cotangent[picked], jnp.zeros((), cotangent.dtype))
        sign_values = sign_table(row_index, col_index, sign_seeds[expert_index], D)
        tangent_grads, curvature = expert_rows(rows_x, rows_cot, w_gate[expert_index], w_up[expert_index], w_down[expert_index], sign_values)
        masked = jnp.where(live_rows[:, None], tangent_grads, jnp.zeros((), jnp.float32))
        accumulated = accumulated.at[picked].add(masked)
        return (accumulated, curvature)
    start_total = jnp.zeros((TOKENS, D), jnp.float32)
    total, curvature = lax.scan(one_expert, start_total, expert_ids)
    return (total.astype(jnp.bfloat16), curvature)
```

```python
import math

import jax
import jax.numpy as jnp
from jax import lax
from jax.sharding import Mesh, PartitionSpec as P

EXPERT = ("x", "z")
SWAP = [(0, 1), (1, 0)]


def mix_bits(row_index, col_index, seed_value):
    mixed = (
        row_index * jnp.int32(73856093)
        + col_index * jnp.int32(19349663)
        + seed_value * jnp.int32(83492791)
    )
    mixed = mixed ^ mixed >> 15
    mixed = mixed * jnp.int32(735632791)
    mixed = mixed ^ mixed >> 13
    mixed = mixed * jnp.int32(1274126177)
    mixed = mixed ^ mixed >> 16
    return mixed >> 5 & 1


def sign_table(row_index, col_index, seed_value, model_width):
    bits = mix_bits(row_index, col_index, seed_value)
    scale = jnp.asarray(1.0 / math.sqrt(model_width), jnp.bfloat16)
    return jnp.where(bits == 1, scale, -scale)


def silu_slopes(pre_act):
    sigmoid_pre = jax.nn.sigmoid(pre_act)
    slope_one = sigmoid_pre * (1.0 + pre_act * (1.0 - sigmoid_pre))
    slope_two = sigmoid_pre * (1.0 - sigmoid_pre) * (2.0 + pre_act * (1.0 - 2.0 * sigmoid_pre))
    return (slope_one, slope_two)


def expert_rows(rows_x, rows_cot, gate_mat, up_mat, down_mat, sign_values):
    contract = (((1,), (1,)), ((), ()))
    gate_pre = jnp.dot(rows_x, gate_mat, preferred_element_type=jnp.float32)
    up_pre = jnp.dot(rows_x, up_mat, preferred_element_type=jnp.float32)
    gate_tangent = jnp.dot(rows_x, sign_values, preferred_element_type=jnp.float32)
    hidden_grad = lax.dot_general(rows_cot, down_mat, contract, preferred_element_type=jnp.float32)
    slope_one, slope_two = silu_slopes(gate_pre)
    grad_gate = (hidden_grad * up_pre * slope_one).astype(jnp.bfloat16)
    tangent_gate = hidden_grad * up_pre * slope_two * gate_tangent
    tangent_up = (hidden_grad * slope_one * gate_tangent).astype(jnp.bfloat16)
    curvature = jnp.sum(gate_tangent * tangent_gate, axis=0)
    tangent_grads = lax.dot_general(
        tangent_gate.astype(jnp.bfloat16), gate_mat, contract, preferred_element_type=jnp.float32
    )
    tangent_grads = tangent_grads + lax.dot_general(
        tangent_up, up_mat, contract, preferred_element_type=jnp.float32
    )
    tangent_grads = tangent_grads + lax.dot_general(
        grad_gate, sign_values, contract, preferred_element_type=jnp.float32
    )
    return (tangent_grads, curvature)


def dispatch_matrix(route_flat, expert_count, slot_count):
    tok_count = route_flat.shape[0]
    place = jnp.arange(tok_count, dtype=jnp.int32)
    earlier = (route_flat[:, None] == route_flat[None, :]) & (place[:, None] < place[None, :])
    slot_place = jnp.sum(earlier.astype(jnp.int32), axis=0)
    target = route_flat * slot_count + slot_place
    slot_ids = jnp.arange(expert_count * slot_count, dtype=jnp.int32)
    return (slot_ids[:, None] == target[None, :]).astype(jnp.bfloat16)


def join_cores(own, core):
    other = lax.ppermute(own, "c", SWAP)
    count = own.shape[0]
    both = jnp.zeros((2 * count,) + own.shape[1:], own.dtype)
    both = lax.dynamic_update_slice_in_dim(both, own, core * count, 0)
    return lax.dynamic_update_slice_in_dim(both, other, (1 - core) * count, 0)


def gather_y(own):
    count = lax.axis_size("y")
    return lax.all_to_all(
        jnp.broadcast_to(own[None], (count,) + own.shape), "y", split_axis=0, concat_axis=0, tiled=True
    )


def body(tokens, cotangent, expert_route, w_gate, w_up, w_down, sign_seeds):
    expert_count = lax.axis_size(EXPERT)
    ys, cores = lax.axis_size("y"), lax.axis_size("c")
    y, core = lax.axis_index("y"), lax.axis_index("c")
    tok_count, model_width = tokens.shape
    hidden_cols = w_gate.shape[2]
    slot_count = max(2, 2 * tok_count // expert_count)
    rows = expert_count * slot_count
    width = model_width // (ys * cores)
    offset = (y * cores + core) * hidden_cols
    row_index = jnp.arange(model_width, dtype=jnp.int32)[:, None]
    col_index = offset + jnp.arange(hidden_cols, dtype=jnp.int32)[None, :]
    sign_values = sign_table(row_index, col_index, sign_seeds[0], model_width)
    dispatch = dispatch_matrix(expert_route[:, 0], expert_count, slot_count)

    start = (core * ys + y) * width
    piece = jnp.concatenate(
        [lax.dynamic_slice_in_dim(a, start, width, 1) for a in (tokens, cotangent)], axis=1
    )
    send = jnp.dot(dispatch, piece, preferred_element_type=jnp.float32).astype(jnp.bfloat16)
    received = lax.all_to_all(
        send.reshape(expert_count, slot_count, 2 * width), EXPERT, split_axis=0, concat_axis=0, tiled=True
    ).reshape(rows, 2 * width)
    blocks = join_cores(gather_y(received), core)
    rows_x = blocks[:, :, :width].transpose(1, 0, 2).reshape(rows, model_width)
    rows_cot = blocks[:, :, width:].transpose(1, 0, 2).reshape(rows, model_width)
    tangent_grads, curvature = expert_rows(
        rows_x, rows_cot, w_gate[0], w_up[0], w_down[0], sign_values
    )

    halves = tangent_grads.reshape(rows, cores, model_width // cores)
    keep = lax.dynamic_slice_in_dim(halves, core, 1, 1)[:, 0]
    give = lax.dynamic_slice_in_dim(halves, 1 - core, 1, 1)[:, 0].astype(jnp.bfloat16)
    pair = keep + lax.ppermute(give, "c", SWAP).astype(jnp.float32)
    parts = pair.astype(jnp.bfloat16).reshape(rows, ys, width).transpose(1, 0, 2)
    parts = lax.all_to_all(parts, "y", split_axis=0, concat_axis=0, tiled=True)
    own_rows = jnp.sum(parts.astype(jnp.float32), axis=0).astype(jnp.bfloat16)
    returned = lax.all_to_all(
        own_rows.reshape(expert_count, slot_count, width), EXPERT, split_axis=0, concat_axis=0, tiled=True
    ).reshape(rows, width)
    combined = lax.dot_general(
        dispatch, returned, (((0,), (0,)), ((), ())), preferred_element_type=jnp.float32
    ).astype(jnp.bfloat16)
    result = join_cores(gather_y(combined), core)
    result = result.transpose(1, 0, 2).reshape(tok_count, model_width)
    return (result, curvature[None, :])


def solution(mesh):
    chips = Mesh(mesh.devices.reshape(4, 8, 4, 2), ("x", "z", "y", "c"))
    expert, dp = EXPERT, ("y", "c")
    in_specs = (
        P(expert, None),
        P(expert, None),
        P(expert, None),
        P(expert, None, dp),
        P(expert, None, dp),
        P(expert, dp, None),
        P(expert),
    )
    out_specs = (P(expert, None), P(expert, dp))
    return jax.shard_map(body, mesh=chips, in_specs=in_specs, out_specs=out_specs, check_vma=False)
```

```python
import functools
import math

import jax
import jax.numpy as jnp
from jax import lax
from jax.experimental import pallas as pl
from jax.experimental.pallas import tpu as pltpu
from jax.sharding import Mesh, PartitionSpec as P

EXPERT = ("x", "z")
SWAP = [(0, 1), (1, 0)]
SHIFTS = (1, -1, 2)
TILE = 256
VMEM = 56 * 1024 * 1024
BF16 = jnp.bfloat16
F32 = jnp.float32


def params():
    return pltpu.CompilerParams(vmem_limit_bytes=VMEM)


def cost(flops, moved, exps=0):
    return pl.CostEstimate(flops=flops, bytes_accessed=moved, transcendentals=exps)


def sign_kernel(info_ref, out_ref):
    rows, cols = out_ref.shape
    first = pl.program_id(0) * rows
    row = lax.broadcasted_iota(jnp.int32, (rows, 1), 0) + first
    col = lax.broadcasted_iota(jnp.int32, (1, cols), 1) + info_ref[0]
    mixed = row * jnp.int32(73856093) + (
        col * jnp.int32(19349663) + info_ref[1] * jnp.int32(83492791)
    )
    mixed = mixed ^ mixed >> 15
    mixed = mixed * jnp.int32(735632791)
    mixed = mixed ^ mixed >> 13
    mixed = mixed * jnp.int32(1274126177)
    mixed = mixed ^ mixed >> 16
    scale = jnp.asarray(1.0 / math.sqrt(2048), BF16).astype(F32)
    out_ref[...] = jnp.where((mixed & 32) != 0, scale, -scale).astype(BF16)


def sign_table(offset, seed, model_width, hidden_cols):
    info = jnp.stack([offset, seed])
    rows = 128
    return pl.pallas_call(
        sign_kernel,
        out_shape=jax.ShapeDtypeStruct((model_width, hidden_cols), BF16),
        grid=(model_width // rows,),
        in_specs=[pl.BlockSpec(memory_space=pltpu.SMEM)],
        out_specs=pl.BlockSpec((rows, hidden_cols), lambda i: (i, 0)),
        compiler_params=params(),
        cost_estimate=cost(30 * model_width * hidden_cols, 2 * model_width * hidden_cols),
        name="sign_table",
    )(info)


def place(scratch, half, blocks_ref, y, ys):
    width = blocks_ref.shape[2]
    for slot, shift in enumerate((0,) + SHIFTS):
        source = lax.rem(y - shift + ys, ys)
        column = pl.multiple_of(half + source * width, width)
        scratch[:, pl.ds(column, width)] = blocks_ref[slot]


def forward_kernel(ys, pos_ref, own_ref, other_ref, gate_ref, up_ref, sign_ref, a_ref, b_ref, c_ref, e_ref, xs):
    y, core = pos_ref[0], pos_ref[1]
    half = xs.shape[1] // 2

    @pl.when(pl.program_id(0) == 0)
    def _():
        place(xs, core * half, own_ref, y, ys)
        place(xs, (1 - core) * half, other_ref, y, ys)

    x = xs[...]
    pre = jnp.dot(x, gate_ref[0], preferred_element_type=F32)
    lin = jnp.dot(x, up_ref[0], preferred_element_type=F32)
    tangent = jnp.dot(x, sign_ref[...], preferred_element_type=F32)
    sig = jax.nn.sigmoid(pre)
    rest = 1.0 - sig
    slope = sig * (1.0 + pre * rest)
    bend = sig * rest * (2.0 + pre * (1.0 - 2.0 * sig))
    a_ref[...] = lin * slope
    b_ref[...] = slope * tangent
    third = lin * bend * tangent
    c_ref[...] = third
    e_ref[...] = third * tangent


def forward(pos, own, other, w_gate, w_up, signs):
    ys, rows, width = own.shape
    model, hidden = signs.shape
    whole = pl.BlockSpec((ys, rows, width), lambda j, p: (0, 0, 0))
    weight = pl.BlockSpec((1, model, TILE), lambda j, p: (0, 0, j))
    column = pl.BlockSpec((rows, TILE), lambda j, p: (0, j))
    return pl.pallas_call(
        functools.partial(forward_kernel, ys),
        out_shape=[jax.ShapeDtypeStruct((rows, hidden), F32)] * 4,
        grid_spec=pltpu.PrefetchScalarGridSpec(
            num_scalar_prefetch=1,
            grid=(pl.cdiv(hidden, TILE),),
            in_specs=[whole, whole, weight, weight, pl.BlockSpec((model, TILE), lambda j, p: (0, j))],
            out_specs=[column] * 4,
            scratch_shapes=[pltpu.VMEM((rows, model), BF16)],
        ),
        compiler_params=params(),
        cost_estimate=cost(6 * rows * model * hidden, 6 * model * hidden + 16 * rows * hidden, rows * hidden),
        name="forward",
    )(pos, own, other, w_gate, w_up, signs)


NT = (((1,), (1,)), ((), ()))


def first_half_kernel(ys, pos_ref, own_ref, down_ref, h_ref, cs):
    @pl.when(pl.program_id(0) == 0)
    def _():
        place(cs, 0, own_ref, pos_ref[0], ys)

    h_ref[...] = lax.dot_general(cs[...], down_ref[0], NT, preferred_element_type=F32)


def first_half(pos, own, w_down):
    ys, rows, width = own.shape
    hidden, model = w_down.shape[1:]
    half = model // 2
    return pl.pallas_call(
        functools.partial(first_half_kernel, ys),
        out_shape=jax.ShapeDtypeStruct((rows, hidden), F32),
        grid_spec=pltpu.PrefetchScalarGridSpec(
            num_scalar_prefetch=1,
            grid=(pl.cdiv(hidden, TILE),),
            in_specs=[
                pl.BlockSpec((ys, rows, width), lambda j, p: (0, 0, 0)),
                pl.BlockSpec((1, TILE, half), lambda j, p: (0, j, p[1])),
            ],
            out_specs=pl.BlockSpec((rows, TILE), lambda j, p: (0, j)),
            scratch_shapes=[pltpu.VMEM((rows, half), BF16)],
        ),
        compiler_params=params(),
        cost_estimate=cost(2 * rows * half * hidden, 2 * half * hidden + 4 * rows * hidden),
        name="first_half",
    )(pos, own, w_down)


def middle_kernel(ys, pos_ref, other_ref, down_ref, h_ref, a_ref, b_ref, c_ref, e_ref, tg_ref, tu_ref, gg_ref, cu_ref, cs):
    @pl.when(pl.program_id(0) == 0)
    def _():
        place(cs, 0, other_ref, pos_ref[0], ys)

    h = h_ref[...] + lax.dot_general(cs[...], down_ref[0], NT, preferred_element_type=F32)
    tg_ref[...] = (h * c_ref[...]).astype(BF16)
    tu_ref[...] = (h * b_ref[...]).astype(BF16)
    gg_ref[...] = (h * a_ref[...]).astype(BF16)
    cu_ref[...] = jnp.sum(h * e_ref[...], axis=0, keepdims=True)


def middle(pos, other, w_down, h, factors):
    ys, rows, width = other.shape
    hidden, model = w_down.shape[1:]
    half = model // 2
    column = pl.BlockSpec((rows, TILE), lambda j, p: (0, j))
    return pl.pallas_call(
        functools.partial(middle_kernel, ys),
        out_shape=[jax.ShapeDtypeStruct((rows, hidden), BF16)] * 3 + [jax.ShapeDtypeStruct((1, hidden), F32)],
        grid_spec=pltpu.PrefetchScalarGridSpec(
            num_scalar_prefetch=1,
            grid=(pl.cdiv(hidden, TILE),),
            in_specs=[
                pl.BlockSpec((ys, rows, width), lambda j, p: (0, 0, 0)),
                pl.BlockSpec((1, TILE, half), lambda j, p: (0, j, 1 - p[1])),
                column,
                column,
                column,
                column,
                column,
            ],
            out_specs=[column, column, column, pl.BlockSpec((1, TILE), lambda j, p: (0, j))],
            scratch_shapes=[pltpu.VMEM((rows, half), BF16)],
        ),
        compiler_params=params(),
        cost_estimate=cost(2 * rows * half * hidden, 2 * half * hidden + 26 * rows * hidden),
        name="middle",
    )(pos, other, w_down, h, *factors)


def backward_kernel(pos_ref, tg_ref, tu_ref, gg_ref, gate_ref, up_ref, sign_ref, out_ref):
    total = lax.dot_general(tg_ref[...], gate_ref[0], NT, preferred_element_type=F32)
    total += lax.dot_general(tu_ref[...], up_ref[0], NT, preferred_element_type=F32)
    total += lax.dot_general(gg_ref[...], sign_ref[...], NT, preferred_element_type=F32)
    out_ref[0] = total.astype(out_ref.dtype)


def backward(pos, grads, w_gate, w_up, signs, ys, dtype, flip, name):
    rows, hidden = grads[0].shape
    model = signs.shape[0]
    width = model // (2 * ys)

    def tile(i, p):
        shift = jnp.where(i == 1, 1, jnp.where(i == 2, ys - 1, jnp.where(i == 3, 2, 0)))
        core = 1 - p[1] if flip else p[1]
        return core * ys + lax.rem(p[0] + shift, ys)

    grad = pl.BlockSpec((rows, hidden), lambda i, p: (0, 0))
    weight = pl.BlockSpec((1, width, hidden), lambda i, p: (0, tile(i, p), 0))
    return pl.pallas_call(
        backward_kernel,
        out_shape=jax.ShapeDtypeStruct((ys, rows, width), dtype),
        grid_spec=pltpu.PrefetchScalarGridSpec(
            num_scalar_prefetch=1,
            grid=(ys,),
            in_specs=[grad] * 3 + [weight, weight, pl.BlockSpec((width, hidden), lambda i, p: (tile(i, p), 0))],
            out_specs=pl.BlockSpec((1, rows, width), lambda i, p: (i, 0, 0)),
        ),
        compiler_params=params(),
        cost_estimate=cost(3 * rows * model * hidden, 3 * model * hidden + 6 * rows * hidden),
        name=name,
    )(pos, *grads, w_gate, w_up, signs)


def assemble_kernel(ys, pos_ref, own_ref, other_ref, out_ref):
    y, core = pos_ref[0], pos_ref[1]
    half = out_ref.shape[1] // 2
    place(out_ref, core * half, own_ref, y, ys)
    place(out_ref, (1 - core) * half, other_ref, y, ys)


def assemble(pos, own, other):
    ys, rows, width = own.shape
    return pl.pallas_call(
        functools.partial(assemble_kernel, ys),
        out_shape=jax.ShapeDtypeStruct((rows, 2 * ys * width), own.dtype),
        in_specs=[pl.BlockSpec(memory_space=pltpu.SMEM)] + [pl.BlockSpec(memory_space=pltpu.VMEM)] * 2,
        out_specs=pl.BlockSpec(memory_space=pltpu.VMEM),
        compiler_params=params(),
        cost_estimate=cost(0, 8 * ys * rows * width),
        name="assemble",
    )(pos, own, other)


def shift_y(value, shift):
    count = lax.axis_size("y")
    return lax.ppermute(value, "y", [(i, (i + shift) % count) for i in range(count)])


def gather_y(own):
    return jnp.stack([own] + [shift_y(own, shift) for shift in SHIFTS])


def swap_cores(value):
    return lax.ppermute(value, "c", SWAP)


def exchange(value):
    return lax.all_to_all(value, EXPERT, split_axis=0, concat_axis=0, tiled=True)


def dispatch_matrix(route_flat, expert_count, slot_count):
    tok_count = route_flat.shape[0]
    token = jnp.arange(tok_count, dtype=jnp.int32)
    earlier = (route_flat[:, None] == route_flat[None, :]) & (token[:, None] < token[None, :])
    slot_place = jnp.sum(earlier.astype(jnp.int32), axis=0)
    target = route_flat * slot_count + slot_place
    slot_ids = jnp.arange(expert_count * slot_count, dtype=jnp.int32)
    return (slot_ids[:, None] == target[None, :]).astype(BF16)


def body(tokens, cotangent, expert_route, w_gate, w_up, w_down, sign_seeds):
    expert_count = lax.axis_size(EXPERT)
    ys, cores = lax.axis_size("y"), lax.axis_size("c")
    y, core = lax.axis_index("y"), lax.axis_index("c")
    tok_count, model_width = tokens.shape
    hidden_cols = w_gate.shape[2]
    slot_count = max(2, 2 * tok_count // expert_count)
    rows = expert_count * slot_count
    width = model_width // (ys * cores)
    pos = jnp.stack([y, core]).astype(jnp.int32)
    dispatch = dispatch_matrix(expert_route[:, 0], expert_count, slot_count)

    def send_rows(values):
        piece = lax.dynamic_slice_in_dim(values, (core * ys + y) * width, width, 1)
        send = jnp.dot(dispatch, piece, preferred_element_type=F32).astype(BF16)
        return exchange(send.reshape(expert_count, slot_count, width)).reshape(rows, width)

    x_rows, cotangent = lax.optimization_barrier((send_rows(tokens), cotangent))
    x_moved = [shift_y(x_rows, shift) for shift in SHIFTS]
    cot_rows = send_rows(cotangent)
    x_moved, cot_rows, seed = lax.optimization_barrier((x_moved, cot_rows, sign_seeds[0]))
    x_own = jnp.stack([x_rows] + x_moved)
    x_other = swap_cores(x_own)
    cot_moved = [shift_y(cot_rows, shift) for shift in SHIFTS]
    signs = sign_table((y * cores + core) * hidden_cols, seed, model_width, hidden_cols)
    factors = forward(pos, x_own, x_other, w_gate, w_up, signs)
    factors, cot_moved = lax.optimization_barrier((factors, cot_moved))
    cot_own = jnp.stack([cot_rows] + cot_moved)
    h = first_half(pos, cot_own, w_down)
    *grads, curvature = middle(pos, swap_cores(cot_own), w_down, h, factors)

    give = backward(pos, grads, w_gate, w_up, signs, ys, BF16, True, "backward_give")
    keep = backward(pos, grads, w_gate, w_up, signs, ys, F32, False, "backward_keep")
    pair = keep + swap_cores(give).astype(F32)
    total = pair[0]
    for slot, shift in enumerate(SHIFTS):
        total = total + shift_y(pair[slot + 1].astype(BF16), shift).astype(F32)
    returned = exchange(total.astype(BF16).reshape(expert_count, slot_count, width)).reshape(rows, width)
    combined = lax.dot_general(
        dispatch, returned, (((0,), (0,)), ((), ())), preferred_element_type=F32
    ).astype(BF16)
    result = gather_y(combined)
    return (assemble(pos, result, swap_cores(result)), curvature)


def solution(mesh):
    chips = Mesh(mesh.devices.reshape(4, 8, 4, 2), ("x", "z", "y", "c"))
    expert, dp = EXPERT, ("y", "c")
    in_specs = (
        P(expert, None),
        P(expert, None),
        P(expert, None),
        P(expert, None, dp),
        P(expert, None, dp),
        P(expert, dp, None),
        P(expert),
    )
    out_specs = (P(expert, None), P(expert, dp))
    return jax.shard_map(body, mesh=chips, in_specs=in_specs, out_specs=out_specs, check_vma=False)
```

```python
import math

import jax
import jax.numpy as jnp
from jax import lax
from jax.experimental import pallas as pl
from jax.experimental.pallas import tpu as pltpu
from jax.sharding import Mesh, PartitionSpec as P

EXPERT = ("x", "z")
SWAP = [(0, 1), (1, 0)]
BF16 = jnp.bfloat16
F32 = jnp.float32


def sign_kernel(info_ref, out_ref):
    rows, cols = out_ref.shape
    first = pl.program_id(0) * rows
    col = lax.broadcasted_iota(jnp.int32, (1, cols), 1) + info_ref[0]
    base = col * jnp.int32(19349663) + info_ref[1] * jnp.int32(83492791)
    scale = jnp.asarray(1.0 / math.sqrt(2048), BF16).astype(F32)
    step = 8
    for at in range(0, rows, step):
        row = lax.broadcasted_iota(jnp.int32, (step, 1), 0) + (first + at)
        mixed = row * jnp.int32(73856093) + base
        mixed = mixed ^ mixed >> 15
        mixed = mixed * jnp.int32(735632791)
        mixed = mixed ^ mixed >> 13
        mixed = mixed * jnp.int32(1274126177)
        mixed = mixed ^ mixed >> 16
        out_ref[at : at + step, :] = jnp.where((mixed & 32) != 0, scale, -scale).astype(BF16)


def sign_table(offset, seed, model_width, hidden_cols):
    rows = 512
    return pl.pallas_call(
        sign_kernel,
        out_shape=jax.ShapeDtypeStruct((model_width, hidden_cols), BF16),
        grid=(model_width // rows,),
        in_specs=[pl.BlockSpec(memory_space=pltpu.SMEM)],
        out_specs=pl.BlockSpec((rows, hidden_cols), lambda i: (i, 0)),
        compiler_params=pltpu.CompilerParams(vmem_limit_bytes=8 * 1024 * 1024),
        cost_estimate=pl.CostEstimate(flops=0, bytes_accessed=2 * model_width * hidden_cols, transcendentals=0),
        name="sign_table",
    )(jnp.stack([offset, seed]))


def dot(a, b, ca, cb):
    return lax.dot_general(a, b, (((ca,), (cb,)), ((), ())), preferred_element_type=F32)


def shift_y(value, shift):
    count = lax.axis_size("y")
    return lax.ppermute(value, "y", [(i, (i + shift) % count) for i in range(count)])


def turn(pieces, y):
    count = len(pieces)
    result = jnp.zeros((count,) + pieces[0].shape, pieces[0].dtype)
    for step, piece in enumerate(pieces):
        result = lax.dynamic_update_index_in_dim(result, piece, lax.rem(y + step, count), 0)
    return result


def swap_cores(value):
    return lax.ppermute(value, "c", SWAP)


def exchange(value):
    return lax.all_to_all(value, EXPERT, split_axis=0, concat_axis=0, tiled=True)


def half_of(value, core, axis):
    size = value.shape[axis] // 2
    return lax.dynamic_slice_in_dim(value, core * size, size, axis)


def forward_factors(pre, lin, tangent):
    sig = jax.nn.sigmoid(pre)
    rest = 1.0 - sig
    slope = sig * (1.0 + pre * rest)
    bend = sig * rest * (2.0 + pre * (1.0 - 2.0 * sig))
    third = lin * bend * tangent
    return (lin * slope, slope * tangent, third, third * tangent)


def dispatch_matrix(route_flat, expert_count, slot_count):
    tok_count = route_flat.shape[0]
    token = jnp.arange(tok_count, dtype=jnp.int32)
    earlier = (route_flat[:, None] == route_flat[None, :]) & (token[:, None] < token[None, :])
    slot_place = jnp.sum(earlier.astype(jnp.int32), axis=0)
    target = route_flat * slot_count + slot_place
    slot_ids = jnp.arange(expert_count * slot_count, dtype=jnp.int32)
    return (slot_ids[:, None] == target[None, :]).astype(BF16)


def body(tokens, cotangent, expert_route, w_gate, w_up, w_down, sign_seeds):
    expert_count = lax.axis_size(EXPERT)
    ys, cores = lax.axis_size("y"), lax.axis_size("c")
    y, core = lax.axis_index("y"), lax.axis_index("c")
    tok_count, model_width = tokens.shape
    hidden_cols = w_gate.shape[2]
    slot_count = max(2, 2 * tok_count // expert_count)
    rows = expert_count * slot_count
    width = model_width // (ys * cores)
    half = ys * width
    gate, up, down = w_gate[0], w_up[0], w_down[0]
    dispatch = dispatch_matrix(expert_route[:, 0], expert_count, slot_count)
    barrier = lax.optimization_barrier

    def packed(values):
        piece = lax.dynamic_slice_in_dim(values, (core * ys + y) * width, width, 1)
        send = jnp.dot(dispatch, piece, preferred_element_type=F32).astype(BF16)
        return send.reshape(expert_count, slot_count, width)

    def moved(piece):
        return [shift_y(piece, shift) for shift in (-1, 2, 1)]

    send_x, send_cot = barrier((packed(tokens), packed(cotangent)))
    x_piece, send_cot = barrier((exchange(send_x).reshape(rows, width).T, send_cot))
    x_moved = moved(x_piece)
    cot_piece = exchange(send_cot).reshape(rows, width).T
    x_moved, cot_piece, seed = barrier((x_moved, cot_piece, sign_seeds[0]))
    x_own = turn([x_piece] + x_moved, y).reshape(half, rows)
    x_other = swap_cores(x_own)
    cot_moved = moved(cot_piece)
    signs = sign_table((y * cores + core) * hidden_cols, seed, model_width, hidden_cols)
    mats = (gate, up, signs)
    firsts = barrier([dot(half_of(w, core, 0), x_own, 0, 0) for w in mats])
    factors = forward_factors(*[a + dot(half_of(w, 1 - core, 0), x_other, 0, 0) for a, w in zip(firsts, mats)])
    factors, cot_moved = barrier((factors, cot_moved))
    cot_own = turn([cot_piece] + cot_moved, y).reshape(half, rows)
    cot_other = swap_cores(cot_own)
    first = barrier(dot(half_of(down, core, 1), cot_own, 1, 0))
    h = first + dot(half_of(down, 1 - core, 1), cot_other, 1, 0)
    ggate, tup, tgate = [(h * f).astype(BF16) for f in factors[:3]]
    curvature = jnp.sum(h * factors[3], axis=1)

    def tangent_half(which):
        return (
            dot(half_of(gate, which, 0), tgate, 1, 0)
            + dot(half_of(up, which, 0), tup, 1, 0)
            + dot(half_of(signs, which, 0), ggate, 1, 0)
        )

    give = tangent_half(1 - core).astype(BF16)
    pair = tangent_half(core) + swap_cores(give).astype(F32)

    def part(shift):
        return lax.dynamic_slice_in_dim(pair, lax.rem(y + shift, ys) * width, width, 0)

    total = part(0)
    for shift in (2, 1, 3):
        total = total + shift_y(part(shift).astype(BF16), shift).astype(F32)
    back = total.astype(BF16).T.reshape(expert_count, slot_count, width)
    returned = exchange(back).reshape(rows, width)
    combined = dot(dispatch, returned, 0, 0).astype(BF16)
    own = jnp.stack([combined] + moved(combined))
    result = jnp.zeros((tok_count, model_width), BF16)
    for blocks, of_core in ((own, core), (swap_cores(own), 1 - core)):
        for step in range(ys):
            at = (of_core * ys + lax.rem(y + step, ys)) * width
            result = lax.dynamic_update_slice_in_dim(result, blocks[step], at, 1)
    return (result, curvature[None, :])


def solution(mesh):
    chips = Mesh(mesh.devices.reshape(4, 8, 4, 2), ("x", "z", "y", "c"))
    expert, dp = EXPERT, ("y", "c")
    in_specs = (
        P(expert, None),
        P(expert, None),
        P(expert, None),
        P(expert, None, dp),
        P(expert, None, dp),
        P(expert, dp, None),
        P(expert),
    )
    out_specs = (P(expert, None), P(expert, dp))
    return jax.shard_map(body, mesh=chips, in_specs=in_specs, out_specs=out_specs, check_vma=False)
```

```python
import functools
import math

import jax
import jax.numpy as jnp
from jax import lax
from jax.experimental import pallas as pl
from jax.experimental.pallas import tpu as pltpu
from jax.sharding import Mesh, PartitionSpec as P

EXPERT = ("x", "z")
SWAP = [(0, 1), (1, 0)]
BF16 = jnp.bfloat16
F32 = jnp.float32
VMEM = 63 * 1024 * 1024


ORDER = (2, 1, 3, 0)


def dispatch_kernel(route_ref, tokens_ref, cot_ref, dispatch_ref, send_ref, pieces, sems):
    count = route_ref.shape[1]
    slots, width = dispatch_ref.shape[0], send_ref.shape[1] // 2
    slot_count = slots // lax.axis_size(EXPERT)
    start = (lax.axis_index("c") * lax.axis_size("y") + lax.axis_index("y")) * width
    columns = pl.ds(pl.multiple_of(start, width), width)
    copies = [
        pltpu.make_async_copy(ref.at[:, columns], pieces.at[:, pl.ds(at * width, width)], sems.at[at])
        for at, ref in enumerate((tokens_ref, cot_ref))
    ]
    for copy in copies:
        copy.start()
    across = jnp.broadcast_to(route_ref[...], (count, count))
    down = across.T
    earlier = (down == across) & (
        lax.broadcasted_iota(jnp.int32, (count, count), 0) < lax.broadcasted_iota(jnp.int32, (count, count), 1)
    )
    place = jnp.sum(jnp.where(earlier, 1.0, 0.0), axis=0, keepdims=True).astype(jnp.int32)
    target = route_ref[...] * slot_count + place
    slot = lax.broadcasted_iota(jnp.int32, (slots, count), 0)
    dispatch = jnp.where(slot == target, 1.0, 0.0).astype(BF16)
    dispatch_ref[...] = dispatch
    for copy in copies:
        copy.wait()
    send_ref[...] = jnp.dot(dispatch, pieces[...], preferred_element_type=F32).astype(BF16)


def dispatch_rows(route, tokens, cotangent, slots, width):
    count = tokens.shape[0]
    vmem = pl.BlockSpec(memory_space=pltpu.VMEM)
    anywhere = pl.BlockSpec(memory_space=pl.ANY)
    return pl.pallas_call(
        dispatch_kernel,
        out_shape=[jax.ShapeDtypeStruct((slots, count), BF16), jax.ShapeDtypeStruct((slots, 2 * width), BF16)],
        in_specs=[vmem, anywhere, anywhere],
        out_specs=[vmem, vmem],
        scratch_shapes=[pltpu.VMEM((count, 2 * width), BF16), pltpu.SemaphoreType.DMA((2,))],
        compiler_params=pltpu.CompilerParams(vmem_limit_bytes=VMEM),
        name="dispatch",
    )(route.reshape(1, count), tokens, cotangent)


def stage_kernel(info_ref, gate_ref, up_ref, down_ref, gate_out, up_out, down_out, sign_out, *, block_of):
    rows, cols = sign_out.shape
    gate_out[...] = gate_ref[0]
    up_out[...] = up_ref[0]
    down_out[...] = down_ref[0]
    first = block_of(pl.program_id(0), info_ref) * rows
    col = lax.broadcasted_iota(jnp.int32, (1, cols), 1) + info_ref[2]
    base = col * jnp.int32(19349663) + info_ref[3] * jnp.int32(83492791)
    scale = jnp.asarray(1.0 / math.sqrt(2048), BF16).astype(F32)
    step = 8
    for at in range(0, rows, step):
        row = lax.broadcasted_iota(jnp.int32, (step, 1), 0) + (first + at)
        mixed = row * jnp.int32(73856093) + base
        mixed = mixed ^ mixed >> 15
        mixed = mixed * jnp.int32(735632791)
        mixed = mixed ^ mixed >> 13
        mixed = mixed * jnp.int32(1274126177)
        mixed = mixed ^ mixed >> 16
        sign_out[at : at + step, :] = jnp.where((mixed & 32) != 0, scale, -scale).astype(BF16)


def stage_weights(info, w_gate, w_up, w_down, ys, width):
    model, hidden = w_gate.shape[1:]

    def block_of(i, p):
        k = lax.rem(i, ys)
        shift = jnp.where(k == 0, ORDER[0], jnp.where(k == 1, ORDER[1], jnp.where(k == 2, ORDER[2], ORDER[3])))
        core_of = jnp.where(i < ys, p[1], 1 - p[1])
        return core_of * ys + lax.rem(p[0] + shift, ys)

    rows_in = pl.BlockSpec((1, width, hidden), lambda i, p: (0, block_of(i, p), 0))
    rows_out = pl.BlockSpec((width, hidden), lambda i, p: (i, 0))
    return pl.pallas_call(
        functools.partial(stage_kernel, block_of=block_of),
        out_shape=[
            jax.ShapeDtypeStruct((model, hidden), BF16),
            jax.ShapeDtypeStruct((model, hidden), BF16),
            jax.ShapeDtypeStruct((hidden, model), BF16),
            jax.ShapeDtypeStruct((model, hidden), BF16),
        ],
        grid_spec=pltpu.PrefetchScalarGridSpec(
            num_scalar_prefetch=1,
            grid=(2 * ys,),
            in_specs=[rows_in, rows_in, pl.BlockSpec((1, hidden, width), lambda i, p: (0, 0, block_of(i, p)))],
            out_specs=[rows_out, rows_out, pl.BlockSpec((hidden, width), lambda i, p: (0, i)), rows_out],
        ),
        compiler_params=pltpu.CompilerParams(vmem_limit_bytes=VMEM),
        cost_estimate=pl.CostEstimate(flops=0, bytes_accessed=14 * model * hidden, transcendentals=0),
        name="stage_weights",
    )(info, w_gate, w_up, w_down)


def dot(a, b, ca, cb):
    return lax.dot_general(a, b, (((ca,), (cb,)), ((), ())), preferred_element_type=F32)


def shift_y(value, shift):
    count = lax.axis_size("y")
    return lax.ppermute(value, "y", [(i, (i + shift) % count) for i in range(count)])


def swap_cores(value):
    return lax.ppermute(value, "c", SWAP)


def exchange(value):
    return lax.all_to_all(value, EXPERT, split_axis=0, concat_axis=0, tiled=True)


def forward_factors(pre, lin, tangent):
    sig = jax.nn.sigmoid(pre)
    rest = 1.0 - sig
    slope = sig * (1.0 + pre * rest)
    bend = sig * rest * (2.0 + pre * (1.0 - 2.0 * sig))
    third = lin * bend * tangent
    return (lin * slope, slope * tangent, third, third * tangent)


def body(tokens, cotangent, expert_route, w_gate, w_up, w_down, sign_seeds):
    expert_count = lax.axis_size(EXPERT)
    ys, cores = lax.axis_size("y"), lax.axis_size("c")
    y, core = lax.axis_index("y"), lax.axis_index("c")
    tok_count, model_width = tokens.shape
    hidden_cols = w_gate.shape[2]
    slot_count = max(2, 2 * tok_count // expert_count)
    rows = expert_count * slot_count
    width = model_width // (ys * cores)
    half = ys * width
    barrier = lax.optimization_barrier

    def to_experts(send):
        return exchange(send.reshape(expert_count, slot_count, -1)).reshape(rows, -1)

    def gather_y(piece):
        return [piece if step == 0 else shift_y(piece, ys - step) for step in ORDER]

    dispatch, send = dispatch_rows(expert_route, tokens, cotangent, rows, width)
    send, seed = barrier((send, sign_seeds[0]))
    info = jnp.stack([y, core, (y * cores + core) * hidden_cols, seed]).astype(jnp.int32)
    gate, up, down, signs = stage_weights(info, w_gate, w_up, w_down, ys, width)
    received, gate, up, down, signs = barrier((to_experts(send), gate, up, down, signs))
    x_pieces = gather_y(received[:, :width].T)
    x_pieces, cot_piece = barrier((x_pieces, received[:, width:].T))
    x_own = jnp.concatenate(x_pieces, axis=0)
    x = jnp.concatenate([x_own, swap_cores(x_own)], axis=0)
    cot_pieces = gather_y(cot_piece)
    factors = forward_factors(*[dot(w, x, 0, 0) for w in (gate, up, signs)])
    factors, cot_pieces = barrier((factors, cot_pieces))
    cot_own = jnp.concatenate(cot_pieces, axis=0)
    cot_other = swap_cores(cot_own)
    first = barrier(dot(down[:, :half], cot_own, 1, 0))
    h = first + dot(down[:, half:], cot_other, 1, 0)
    ggate, tup, tgate = [(h * f).astype(BF16) for f in factors[:3]]
    curvature = jnp.sum(h * factors[3], axis=1)

    def tangent(grads, start, stop):
        return sum(dot(w[start:stop], g, 1, 0) for w, g in zip((gate, up, signs), grads))

    def pairs(grads, start, stop):
        give = tangent(grads, half + start, half + stop).astype(BF16)
        return tangent(grads, start, stop) + swap_cores(give).astype(F32)

    grads = (tgate, tup, ggate)
    far, grads = barrier((pairs(grads, 0, width), grads))
    near = pairs(grads, width, half)
    total = near[(ys - 2) * width :] + shift_y(far.astype(BF16), ORDER[0]).astype(F32)
    for at in range(ys - 2):
        total = total + shift_y(near[at * width : (at + 1) * width].astype(BF16), ORDER[at + 1]).astype(F32)
    returned = to_experts(total.astype(BF16).T)
    combined = dot(dispatch, returned, 0, 0).astype(BF16)
    own = jnp.stack(gather_y(combined))
    result = jnp.zeros((tok_count, model_width), BF16)
    for blocks, of_core in ((own, core), (swap_cores(own), 1 - core)):
        for at, step in enumerate(ORDER):
            column = (of_core * ys + lax.rem(y + step, ys)) * width
            result = lax.dynamic_update_slice_in_dim(result, blocks[at], column, 1)
    return (result, curvature[None, :])


def solution(mesh):
    chips = Mesh(mesh.devices.reshape(4, 8, 4, 2), ("x", "z", "y", "c"))
    expert, dp = EXPERT, ("y", "c")
    in_specs = (
        P(expert, None),
        P(expert, None),
        P(expert, None),
        P(expert, None, dp),
        P(expert, None, dp),
        P(expert, dp, None),
        P(expert),
    )
    out_specs = (P(expert, None), P(expert, dp))
    return jax.shard_map(body, mesh=chips, in_specs=in_specs, out_specs=out_specs, check_vma=False)
```

```python
import functools
import math

import jax
import jax.numpy as jnp
from jax import lax
from jax.experimental import pallas as pl
from jax.experimental.pallas import tpu as pltpu
from jax.sharding import Mesh, PartitionSpec as P

EXPERT = ("x", "z")
SWAP = [(0, 1), (1, 0)]
BF16 = jnp.bfloat16
F32 = jnp.float32
VMEM = 63 * 1024 * 1024


BLOCKS = ((0, 2), (1, 2), (0, 1), (0, 3), (0, 0), (1, 1), (1, 3), (1, 0))


def dispatch_kernel(route_ref, tokens_ref, cot_ref, dispatch_ref, send_ref, pieces, sems):
    count = route_ref.shape[1]
    slots, width = dispatch_ref.shape[0], send_ref.shape[1] // 2
    slot_count = slots // lax.axis_size(EXPERT)
    start = (lax.axis_index("c") * lax.axis_size("y") + lax.axis_index("y")) * width
    columns = pl.ds(pl.multiple_of(start, width), width)
    copies = [
        pltpu.make_async_copy(ref.at[:, columns], pieces.at[:, pl.ds(at * width, width)], sems.at[at])
        for at, ref in enumerate((tokens_ref, cot_ref))
    ]
    for copy in copies:
        copy.start()
    across = jnp.broadcast_to(route_ref[...], (count, count))
    down = across.T
    earlier = (down == across) & (
        lax.broadcasted_iota(jnp.int32, (count, count), 0) < lax.broadcasted_iota(jnp.int32, (count, count), 1)
    )
    place = jnp.sum(jnp.where(earlier, 1.0, 0.0), axis=0, keepdims=True).astype(jnp.int32)
    target = route_ref[...] * slot_count + place
    slot = lax.broadcasted_iota(jnp.int32, (slots, count), 0)
    dispatch = jnp.where(slot == target, 1.0, 0.0).astype(BF16)
    dispatch_ref[...] = dispatch
    for copy in copies:
        copy.wait()
    send_ref[...] = jnp.dot(dispatch, pieces[...], preferred_element_type=F32).astype(BF16)


def dispatch_rows(route, tokens, cotangent, slots, width):
    count = tokens.shape[0]
    vmem = pl.BlockSpec(memory_space=pltpu.VMEM)
    hbm = pl.BlockSpec(memory_space=pltpu.HBM)
    return pl.pallas_call(
        dispatch_kernel,
        out_shape=[jax.ShapeDtypeStruct((slots, count), BF16), jax.ShapeDtypeStruct((slots, 2 * width), BF16)],
        in_specs=[vmem, hbm, hbm],
        out_specs=[vmem, vmem],
        scratch_shapes=[pltpu.VMEM((count, 2 * width), BF16), pltpu.SemaphoreType.DMA((2,))],
        compiler_params=pltpu.CompilerParams(vmem_limit_bytes=24 * 1024 * 1024),
        name="dispatch",
    )(route.reshape(1, count), *[pltpu.with_memory_space_constraint(a, pltpu.HBM) for a in (tokens, cotangent)])


def stage_kernel(seed_ref, gate_ref, up_ref, down_ref, mats_ref, cuts_ref, sems):
    hidden = gate_ref.shape[2]
    ys = lax.axis_size("y")
    y, core = lax.axis_index("y"), lax.axis_index("c")
    width = mats_ref.shape[0] // len(BLOCKS)

    def block(other, step):
        return lax.rem(core + other, 2) * ys + lax.rem(y + step, ys)

    copies = []
    for at, (other, step) in enumerate(BLOCKS):
        source = pl.ds(pl.multiple_of(block(other, step) * width, width), width)
        target = pl.ds(at * width, width)
        for which, (from_ref, to_ref) in enumerate(
            (
                (gate_ref.at[0, source, :], mats_ref.at[target, pl.ds(0, hidden)]),
                (up_ref.at[0, source, :], mats_ref.at[target, pl.ds(hidden, hidden)]),
                (down_ref.at[0, :, source], cuts_ref.at[:, target]),
            )
        ):
            copies.append(pltpu.make_async_copy(from_ref, to_ref, sems.at[3 * at + which]))
    for copy in copies:
        copy.start()

    offset = (y * lax.axis_size("c") + core) * hidden
    col = lax.broadcasted_iota(jnp.int32, (1, hidden), 1) + offset
    base = col * jnp.int32(19349663) + seed_ref[0] * jnp.int32(83492791)
    scale = jnp.asarray(1.0 / math.sqrt(2048), BF16).astype(F32)
    count = 16

    def signs(at, first, step):
        row = lax.broadcasted_iota(jnp.int32, (count, 1), 0) + (first * width + step * count)
        mixed = row * jnp.int32(73856093) + base
        mixed = mixed ^ mixed >> 15
        mixed = mixed * jnp.int32(735632791)
        mixed = mixed ^ mixed >> 13
        mixed = mixed * jnp.int32(1274126177)
        mixed = mixed ^ mixed >> 16
        target = pl.ds(pl.multiple_of(at * width + step * count, count), count)
        mats_ref[target, 2 * hidden :] = jnp.where((mixed & 32) != 0, scale, -scale).astype(BF16)

    for at, (other, step) in enumerate(BLOCKS):
        first = block(other, step)
        lax.fori_loop(0, width // count, lambda i, _: signs(at, first, i), None, unroll=4)
    for copy in copies:
        copy.wait()


def stage_weights(seed, w_gate, w_up, w_down):
    model, hidden = w_gate.shape[1:]
    vmem = pl.BlockSpec(memory_space=pltpu.VMEM)
    hbm = pl.BlockSpec(memory_space=pltpu.HBM)
    return pl.pallas_call(
        stage_kernel,
        out_shape=[jax.ShapeDtypeStruct((model, 3 * hidden), BF16), jax.ShapeDtypeStruct((hidden, model), BF16)],
        in_specs=[pl.BlockSpec(memory_space=pltpu.SMEM), hbm, hbm, hbm],
        out_specs=[vmem, vmem],
        scratch_shapes=[pltpu.SemaphoreType.DMA((3 * len(BLOCKS),))],
        compiler_params=pltpu.CompilerParams(vmem_limit_bytes=24 * 1024 * 1024),
        cost_estimate=pl.CostEstimate(flops=0, bytes_accessed=14 * model * hidden, transcendentals=0),
        name="stage_weights",
    )(seed, *[pltpu.with_memory_space_constraint(w, pltpu.HBM) for w in (w_gate, w_up, w_down)])


def dot(a, b, ca, cb):
    return lax.dot_general(a, b, (((ca,), (cb,)), ((), ())), preferred_element_type=F32)


def shift_y(value, shift):
    count = lax.axis_size("y")
    return lax.ppermute(value, "y", [(i, (i + shift) % count) for i in range(count)])


def swap_cores(value):
    return lax.ppermute(value, "c", SWAP)


def exchange(value):
    return lax.all_to_all(value, EXPERT, split_axis=0, concat_axis=0, tiled=True)


def forward_factors(pre, lin, tangent):
    sig = jax.nn.sigmoid(pre)
    rest = 1.0 - sig
    slope = sig * (1.0 + pre * rest)
    bend = sig * rest * (2.0 + pre * (1.0 - 2.0 * sig))
    third = lin * bend * tangent
    return (lin * slope, slope * tangent, third, third * tangent)


def body(tokens, cotangent, expert_route, w_gate, w_up, w_down, sign_seeds):
    expert_count = lax.axis_size(EXPERT)
    ys, cores = lax.axis_size("y"), lax.axis_size("c")
    y, core = lax.axis_index("y"), lax.axis_index("c")
    tok_count, model_width = tokens.shape
    hidden_cols = w_gate.shape[2]
    slot_count = max(2, 2 * tok_count // expert_count)
    rows = expert_count * slot_count
    width = model_width // (ys * cores)
    half = ys * width
    barrier = lax.optimization_barrier

    def to_experts(send):
        return exchange(send.reshape(expert_count, slot_count, -1)).reshape(rows, -1)

    def neighbours(piece):
        return [shift_y(piece, -1), shift_y(piece, 1)]

    def beyond(near):
        cut = rows // 2
        return [shift_y(near[0][:, :cut], -1), shift_y(near[1][:, cut:], 1)]

    def both_cores(pieces, axis):
        own = jnp.concatenate(pieces, axis=axis)
        return own, swap_cores(own)

    dispatch, send = dispatch_rows(expert_route, tokens, cotangent, rows, width)
    send, seed = barrier((send, sign_seeds))
    mats, down = stage_weights(seed, w_gate, w_up, w_down)
    received, mats, down = barrier((to_experts(send), mats, down))
    piece = received.T
    near = neighbours(piece)
    far = beyond(near)
    near.append(piece)
    x_near = both_cores([part[:width] for part in near], 0)
    cot_near = both_cores([part[width:] for part in near], 0)
    split = 2 * width
    sums = dot(mats[split:], jnp.concatenate(x_near, axis=0), 0, 0)
    sums, cot_near, far = barrier((sums, cot_near, far))
    far = both_cores(far, 1)
    cot_sum = dot(down[:, split:], jnp.concatenate(cot_near, axis=0), 1, 0)
    sums, far, cot_sum = barrier((sums, far, cot_sum))
    x_far = jnp.concatenate([part[:width] for part in far], axis=0)
    cot_far = jnp.concatenate([part[width:] for part in far], axis=0)
    spans = [slice(at * hidden_cols, (at + 1) * hidden_cols) for at in range(3)]
    factors = forward_factors(*[sums[span] + dot(mats[:split, span], x_far, 0, 0) for span in spans])
    h = cot_sum + dot(down[:, :split], cot_far, 1, 0)
    curvature = jnp.sum(h * factors[3], axis=1)
    grads = jnp.concatenate([(h * f).astype(BF16) for f in (factors[2], factors[1], factors[0])], axis=0)

    def partial(start, count):
        return dot(mats[start * width : (start + count) * width], grads, 1, 0)

    give_far = partial(1, 1).astype(BF16)
    give_far, grads = barrier((give_far, grads))
    give_near = partial(5, 2).astype(BF16)
    swapped = swap_cores(give_far)
    swapped, give_near, grads = barrier((swapped, give_near, grads))
    sum_far = partial(0, 1) + swapped.astype(F32)
    sum_far, grads = barrier((sum_far, grads))
    sum_near = partial(2, 2) + swap_cores(give_near).astype(F32)
    sum_near, grads = barrier((sum_near, grads))
    total = partial(4, 1) + swap_cores(partial(7, 1).astype(BF16)).astype(F32)
    total = total + shift_y(sum_far.astype(BF16), 2).astype(F32)
    for at, shift in enumerate((1, 3)):
        total = total + shift_y(sum_near[at * width : (at + 1) * width].astype(BF16), shift).astype(F32)
    returned = to_experts(total.astype(BF16).T)
    combined = dot(dispatch, returned, 0, 0).astype(BF16)
    steps = (2, 1, 3, 0)
    own = jnp.stack([shift_y(combined, ys - step) for step in steps[:-1]] + [combined])
    result = jnp.zeros((tok_count, model_width), BF16)
    for blocks, of_core in ((own, core), (swap_cores(own), 1 - core)):
        for at, step in enumerate(steps):
            column = (of_core * ys + lax.rem(y + step, ys)) * width
            result = lax.dynamic_update_slice_in_dim(result, blocks[at], column, 1)
    return (result, curvature[None, :])


def solution(mesh):
    chips = Mesh(mesh.devices.reshape(4, 8, 4, 2), ("x", "z", "y", "c"))
    expert, dp = EXPERT, ("y", "c")
    in_specs = (
        P(expert, None),
        P(expert, None),
        P(expert, None),
        P(expert, None, dp),
        P(expert, None, dp),
        P(expert, dp, None),
        P(expert),
    )
    out_specs = (P(expert, None), P(expert, dp))
    return jax.shard_map(body, mesh=chips, in_specs=in_specs, out_specs=out_specs, check_vma=False)
```

```python
import functools
import math

import jax
import jax.numpy as jnp
from jax import lax
from jax.experimental import pallas as pl
from jax.experimental.pallas import tpu as pltpu
from jax.sharding import Mesh, PartitionSpec as P

EXPERT = ("x", "z")
SWAP = [(0, 1), (1, 0)]
BF16 = jnp.bfloat16
F32 = jnp.float32
VMEM = 63 * 1024 * 1024


BLOCKS = ((0, 2), (1, 2), (0, 1), (0, 3), (0, 0), (1, 1), (1, 3), (1, 0))


def dispatch_kernel(route_hbm, tokens_ref, cot_ref, dispatch_ref, send_ref, route_ref, pieces, sems):
    count = route_hbm.shape[1]
    slots, width = dispatch_ref.shape[0], send_ref.shape[1] // 2
    slot_count = slots // lax.axis_size(EXPERT)
    start = (lax.axis_index("c") * lax.axis_size("y") + lax.axis_index("y")) * width
    columns = pl.ds(pl.multiple_of(start, width), width)
    copies = [
        pltpu.make_async_copy(ref.at[:, columns], pieces.at[:, pl.ds(at * width, width)], sems.at[at])
        for at, ref in enumerate((tokens_ref, cot_ref))
    ]
    copies.append(pltpu.make_async_copy(route_hbm, route_ref, sems.at[2]))
    for copy in reversed(copies):
        copy.start()
    copies.pop().wait()
    across = jnp.broadcast_to(route_ref[...], (count, count))
    down = across.T
    earlier = (down == across) & (
        lax.broadcasted_iota(jnp.int32, (count, count), 0) < lax.broadcasted_iota(jnp.int32, (count, count), 1)
    )
    place = jnp.sum(jnp.where(earlier, 1.0, 0.0), axis=0, keepdims=True).astype(jnp.int32)
    target = route_ref[...] * slot_count + place
    slot = lax.broadcasted_iota(jnp.int32, (slots, count), 0)
    dispatch = jnp.where(slot == target, 1.0, 0.0).astype(BF16)
    dispatch_ref[...] = dispatch
    for copy in copies:
        copy.wait()
    send_ref[...] = jnp.dot(dispatch, pieces[...], preferred_element_type=F32).astype(BF16)


def dispatch_rows(route, tokens, cotangent, slots, width):
    count = tokens.shape[0]
    vmem = pl.BlockSpec(memory_space=pltpu.VMEM)
    hbm = pl.BlockSpec(memory_space=pltpu.HBM)
    return pl.pallas_call(
        dispatch_kernel,
        out_shape=[jax.ShapeDtypeStruct((slots, count), BF16), jax.ShapeDtypeStruct((slots, 2 * width), BF16)],
        in_specs=[hbm, hbm, hbm],
        out_specs=[vmem, vmem],
        scratch_shapes=[
            pltpu.VMEM((1, count), jnp.int32),
            pltpu.VMEM((count, 2 * width), BF16),
            pltpu.SemaphoreType.DMA((3,)),
        ],
        compiler_params=pltpu.CompilerParams(vmem_limit_bytes=24 * 1024 * 1024),
        name="dispatch",
    )(*[pltpu.with_memory_space_constraint(a, pltpu.HBM) for a in (route.reshape(1, count), tokens, cotangent)])


def stage_kernel(seed_ref, gate_ref, up_ref, down_ref, mats_ref, cuts_ref, sems):
    hidden = gate_ref.shape[2]
    ys = lax.axis_size("y")
    y, core = lax.axis_index("y"), lax.axis_index("c")
    width = mats_ref.shape[0] // len(BLOCKS)

    def block(other, step):
        return lax.rem(core + other, 2) * ys + lax.rem(y + step, ys)

    copies = []
    for at, (other, step) in enumerate(BLOCKS):
        source = pl.ds(pl.multiple_of(block(other, step) * width, width), width)
        target = pl.ds(at * width, width)
        for which, (from_ref, to_ref) in enumerate(
            (
                (gate_ref.at[0, source, :], mats_ref.at[target, pl.ds(0, hidden)]),
                (up_ref.at[0, source, :], mats_ref.at[target, pl.ds(hidden, hidden)]),
                (down_ref.at[0, :, source], cuts_ref.at[:, target]),
            )
        ):
            copies.append(pltpu.make_async_copy(from_ref, to_ref, sems.at[3 * at + which]))
    for copy in copies:
        copy.start()

    offset = (y * lax.axis_size("c") + core) * hidden
    col = lax.broadcasted_iota(jnp.int32, (1, hidden), 1) + offset
    base = col * jnp.int32(19349663) + seed_ref[0] * jnp.int32(83492791)
    scale = jnp.asarray(1.0 / math.sqrt(2048), BF16).astype(F32)
    count = 16

    def signs(at, first, step):
        row = lax.broadcasted_iota(jnp.int32, (count, 1), 0) + (first * width + step * count)
        mixed = row * jnp.int32(73856093) + base
        mixed = mixed ^ mixed >> 15
        mixed = mixed * jnp.int32(735632791)
        mixed = mixed ^ mixed >> 13
        mixed = mixed * jnp.int32(1274126177)
        mixed = mixed ^ mixed >> 16
        target = pl.ds(pl.multiple_of(at * width + step * count, count), count)
        mats_ref[target, 2 * hidden :] = jnp.where((mixed & 32) != 0, scale, -scale).astype(BF16)

    for at, (other, step) in enumerate(BLOCKS):
        first = block(other, step)
        lax.fori_loop(0, width // count, lambda i, _: signs(at, first, i), None, unroll=4)
    for copy in copies:
        copy.wait()


def stage_weights(seed, w_gate, w_up, w_down):
    model, hidden = w_gate.shape[1:]
    vmem = pl.BlockSpec(memory_space=pltpu.VMEM)
    hbm = pl.BlockSpec(memory_space=pltpu.HBM)
    return pl.pallas_call(
        stage_kernel,
        out_shape=[jax.ShapeDtypeStruct((model, 3 * hidden), BF16), jax.ShapeDtypeStruct((hidden, model), BF16)],
        in_specs=[pl.BlockSpec(memory_space=pltpu.SMEM), hbm, hbm, hbm],
        out_specs=[vmem, vmem],
        scratch_shapes=[pltpu.SemaphoreType.DMA((3 * len(BLOCKS),))],
        compiler_params=pltpu.CompilerParams(vmem_limit_bytes=24 * 1024 * 1024),
        cost_estimate=pl.CostEstimate(flops=0, bytes_accessed=14 * model * hidden, transcendentals=0),
        name="stage_weights",
    )(seed, *[pltpu.with_memory_space_constraint(w, pltpu.HBM) for w in (w_gate, w_up, w_down)])


def dot(a, b, ca, cb):
    return lax.dot_general(a, b, (((ca,), (cb,)), ((), ())), preferred_element_type=F32)


def shift_y(value, shift):
    count = lax.axis_size("y")
    return lax.ppermute(value, "y", [(i, (i + shift) % count) for i in range(count)])


def swap_cores(value):
    return lax.ppermute(value, "c", SWAP)


def exchange(value):
    return lax.all_to_all(value, EXPERT, split_axis=0, concat_axis=0, tiled=True)


def forward_factors(pre, lin, tangent):
    sig = jax.nn.sigmoid(pre)
    rest = 1.0 - sig
    slope = sig * (1.0 + pre * rest)
    bend = sig * rest * (2.0 + pre * (1.0 - 2.0 * sig))
    third = lin * bend * tangent
    return (lin * slope, slope * tangent, third, third * tangent)


def body(tokens, cotangent, expert_route, w_gate, w_up, w_down, sign_seeds):
    expert_count = lax.axis_size(EXPERT)
    ys, cores = lax.axis_size("y"), lax.axis_size("c")
    y, core = lax.axis_index("y"), lax.axis_index("c")
    tok_count, model_width = tokens.shape
    hidden_cols = w_gate.shape[2]
    slot_count = max(2, 2 * tok_count // expert_count)
    rows = expert_count * slot_count
    width = model_width // (ys * cores)
    half = ys * width
    barrier = lax.optimization_barrier

    def to_experts(send):
        return exchange(send.reshape(expert_count, slot_count, -1)).reshape(rows, -1)

    def neighbours(piece):
        return [shift_y(piece, -1), shift_y(piece, 1)]

    def beyond(near):
        cut = rows // 2
        return [shift_y(near[0][:, :cut], -1), shift_y(near[1][:, cut:], 1)]

    def both_cores(pieces, axis):
        own = jnp.concatenate(pieces, axis=axis)
        return own, swap_cores(own)

    dispatch, send = dispatch_rows(expert_route, tokens, cotangent, rows, width)
    received, seed = barrier((to_experts(send), sign_seeds))
    mats, down = stage_weights(seed, w_gate, w_up, w_down)
    piece = received.T
    near = neighbours(piece)
    crossed = swap_cores(piece)
    near, mats, down, crossed = barrier((near, mats, down, crossed))
    x_far = beyond([part[:width] for part in near])
    cot_far = beyond([part[width:] for part in near])
    joint = jnp.concatenate(near, axis=0)
    other = swap_cores(joint)
    near = near + [piece, other[: 2 * width], other[2 * width :], crossed]
    x_near = [part[:width] for part in near]
    cot_near = [part[width:] for part in near]
    split = 2 * width
    sums = dot(mats[split:], jnp.concatenate(x_near, axis=0), 0, 0)
    sums, cot_near, x_far = barrier((sums, cot_near, x_far))
    x_far = jnp.concatenate(both_cores(x_far, 1), axis=0)
    cot_sum = dot(down[:, split:], jnp.concatenate(cot_near, axis=0), 1, 0)
    sums, x_far, cot_sum, cot_far = barrier((sums, x_far, cot_sum, cot_far))
    cot_far = jnp.concatenate(both_cores(cot_far, 1), axis=0)
    spans = [slice(at * hidden_cols, (at + 1) * hidden_cols) for at in range(3)]
    factors = forward_factors(*[sums[span] + dot(mats[:split, span], x_far, 0, 0) for span in spans])
    factors, cot_far = barrier((factors, cot_far))
    h = cot_sum + dot(down[:, :split], cot_far, 1, 0)
    curvature = jnp.sum(h * factors[3], axis=1)
    grads = jnp.concatenate([(h * f).astype(BF16) for f in (factors[2], factors[1], factors[0])], axis=0)

    def partial(start, count):
        return dot(mats[start * width : (start + count) * width], grads, 1, 0)

    give_far = partial(1, 1).astype(BF16)
    give_far, grads = barrier((give_far, grads))
    give_rest = partial(5, 3).astype(BF16)
    swapped = swap_cores(give_far)
    swapped, give_rest, grads = barrier((swapped, give_rest, grads))
    sum_far = partial(0, 1) + swapped.astype(F32)
    sum_far, grads = barrier((sum_far, grads))
    sum_rest = partial(2, 3) + swap_cores(give_rest).astype(F32)
    total = sum_rest[2 * width :] + shift_y(sum_far.astype(BF16), 2).astype(F32)
    for at, shift in enumerate((1, 3)):
        total = total + shift_y(sum_rest[at * width : (at + 1) * width].astype(BF16), shift).astype(F32)
    returned = to_experts(total.astype(BF16).T)
    combined = dot(dispatch, returned, 0, 0).astype(BF16)
    steps = (2, 1, 3, 0)
    own = jnp.stack([shift_y(combined, ys - step) for step in steps[:-1]] + [combined])
    result = jnp.zeros((tok_count, model_width), BF16)
    for blocks, of_core in ((own, core), (swap_cores(own), 1 - core)):
        for at, step in enumerate(steps):
            column = (of_core * ys + lax.rem(y + step, ys)) * width
            result = lax.dynamic_update_slice_in_dim(result, blocks[at], column, 1)
    return (result, curvature[None, :])


def solution(mesh):
    chips = Mesh(mesh.devices.reshape(4, 8, 4, 2), ("x", "z", "y", "c"))
    expert, dp = EXPERT, ("y", "c")
    in_specs = (
        P(expert, None),
        P(expert, None),
        P(expert, None),
        P(expert, None, dp),
        P(expert, None, dp),
        P(expert, dp, None),
        P(expert),
    )
    out_specs = (P(expert, None), P(expert, dp))
    return jax.shard_map(body, mesh=chips, in_specs=in_specs, out_specs=out_specs, check_vma=False)
```

```python
import functools
import math

import jax
import jax.numpy as jnp
from jax import lax
from jax.experimental import pallas as pl
from jax.experimental.pallas import tpu as pltpu
from jax.sharding import Mesh, PartitionSpec as P

EXPERT = ("x", "z")
SWAP = [(0, 1), (1, 0)]
BF16 = jnp.bfloat16
F32 = jnp.float32
VMEM = 63 * 1024 * 1024


BLOCKS = ((0, 2), (1, 2), (0, 1), (0, 3), (0, 0), (1, 1), (1, 3), (1, 0))


def dispatch_kernel(route_hbm, tokens_ref, cot_ref, dispatch_ref, send_ref, route_ref, pieces, sems):
    count = route_hbm.shape[1]
    slots, width = dispatch_ref.shape[0], send_ref.shape[1] // 2
    slot_count = slots // lax.axis_size(EXPERT)
    start = (lax.axis_index("c") * lax.axis_size("y") + lax.axis_index("y")) * width
    columns = pl.ds(pl.multiple_of(start, width), width)
    copies = [
        pltpu.make_async_copy(ref.at[:, columns], pieces.at[:, pl.ds(at * width, width)], sems.at[at])
        for at, ref in enumerate((tokens_ref, cot_ref))
    ]
    copies.append(pltpu.make_async_copy(route_hbm, route_ref, sems.at[2]))
    for copy in reversed(copies):
        copy.start()
    copies.pop().wait()
    across = jnp.broadcast_to(route_ref[...], (count, count))
    down = across.T
    earlier = (down == across) & (
        lax.broadcasted_iota(jnp.int32, (count, count), 0) < lax.broadcasted_iota(jnp.int32, (count, count), 1)
    )
    place = jnp.sum(jnp.where(earlier, 1.0, 0.0), axis=0, keepdims=True).astype(jnp.int32)
    target = route_ref[...] * slot_count + place
    slot = lax.broadcasted_iota(jnp.int32, (slots, count), 0)
    dispatch = jnp.where(slot == target, 1.0, 0.0).astype(BF16)
    dispatch_ref[...] = dispatch
    for copy in copies:
        copy.wait()
    send_ref[...] = jnp.dot(dispatch, pieces[...], preferred_element_type=F32).astype(BF16)


def dispatch_rows(route, tokens, cotangent, slots, width):
    count = tokens.shape[0]
    vmem = pl.BlockSpec(memory_space=pltpu.VMEM)
    hbm = pl.BlockSpec(memory_space=pltpu.HBM)
    return pl.pallas_call(
        dispatch_kernel,
        out_shape=[jax.ShapeDtypeStruct((slots, count), BF16), jax.ShapeDtypeStruct((slots, 2 * width), BF16)],
        in_specs=[hbm, hbm, hbm],
        out_specs=[vmem, vmem],
        scratch_shapes=[
            pltpu.VMEM((1, count), jnp.int32),
            pltpu.VMEM((count, 2 * width), BF16),
            pltpu.SemaphoreType.DMA((3,)),
        ],
        compiler_params=pltpu.CompilerParams(vmem_limit_bytes=24 * 1024 * 1024),
        name="dispatch",
    )(*[pltpu.with_memory_space_constraint(a, pltpu.HBM) for a in (route.reshape(1, count), tokens, cotangent)])


def stage_kernel(seed_ref, gate_ref, up_ref, down_ref, mats_ref, cuts_ref, sems):
    hidden = gate_ref.shape[2]
    ys = lax.axis_size("y")
    y, core = lax.axis_index("y"), lax.axis_index("c")
    width = mats_ref.shape[0] // len(BLOCKS)

    def block(other, step):
        return lax.rem(core + other, 2) * ys + lax.rem(y + step, ys)

    copies = []
    for at, (other, step) in enumerate(BLOCKS):
        source = pl.ds(pl.multiple_of(block(other, step) * width, width), width)
        target = pl.ds(at * width, width)
        for which, (from_ref, to_ref) in enumerate(
            (
                (gate_ref.at[0, source, :], mats_ref.at[target, pl.ds(0, hidden)]),
                (up_ref.at[0, source, :], mats_ref.at[target, pl.ds(hidden, hidden)]),
                (down_ref.at[0, :, source], cuts_ref.at[:, target]),
            )
        ):
            copies.append(pltpu.make_async_copy(from_ref, to_ref, sems.at[3 * at + which]))
    for copy in copies:
        copy.start()

    offset = (y * lax.axis_size("c") + core) * hidden
    col = lax.broadcasted_iota(jnp.int32, (1, hidden), 1) + offset
    base = col * jnp.int32(19349663) + seed_ref[0] * jnp.int32(83492791)
    scale = jnp.asarray(1.0 / math.sqrt(2048), BF16).astype(F32)
    count = 16

    def signs(at, first, step):
        row = lax.broadcasted_iota(jnp.int32, (count, 1), 0) + (first * width + step * count)
        mixed = row * jnp.int32(73856093) + base
        mixed = mixed ^ mixed >> 15
        mixed = mixed * jnp.int32(735632791)
        mixed = mixed ^ mixed >> 13
        mixed = mixed * jnp.int32(1274126177)
        mixed = mixed ^ mixed >> 16
        target = pl.ds(pl.multiple_of(at * width + step * count, count), count)
        mats_ref[target, 2 * hidden :] = jnp.where((mixed & 32) != 0, scale, -scale).astype(BF16)

    for at, (other, step) in enumerate(BLOCKS):
        first = block(other, step)
        lax.fori_loop(0, width // count, lambda i, _: signs(at, first, i), None, unroll=4)
    for copy in copies:
        copy.wait()


def stage_weights(seed, w_gate, w_up, w_down):
    model, hidden = w_gate.shape[1:]
    vmem = pl.BlockSpec(memory_space=pltpu.VMEM)
    hbm = pl.BlockSpec(memory_space=pltpu.HBM)
    return pl.pallas_call(
        stage_kernel,
        out_shape=[jax.ShapeDtypeStruct((model, 3 * hidden), BF16), jax.ShapeDtypeStruct((hidden, model), BF16)],
        in_specs=[pl.BlockSpec(memory_space=pltpu.SMEM), hbm, hbm, hbm],
        out_specs=[vmem, vmem],
        scratch_shapes=[pltpu.SemaphoreType.DMA((3 * len(BLOCKS),))],
        compiler_params=pltpu.CompilerParams(vmem_limit_bytes=24 * 1024 * 1024),
        cost_estimate=pl.CostEstimate(flops=0, bytes_accessed=14 * model * hidden, transcendentals=0),
        name="stage_weights",
    )(seed, *[pltpu.with_memory_space_constraint(w, pltpu.HBM) for w in (w_gate, w_up, w_down)])


def dot(a, b, ca, cb):
    return lax.dot_general(a, b, (((ca,), (cb,)), ((), ())), preferred_element_type=F32)


def shift_y(value, shift):
    count = lax.axis_size("y")
    return lax.ppermute(value, "y", [(i, (i + shift) % count) for i in range(count)])


def swap_cores(value):
    return lax.ppermute(value, "c", SWAP)


def exchange(value):
    return lax.all_to_all(value, EXPERT, split_axis=0, concat_axis=0, tiled=True)


def forward_factors(pre, lin, tangent):
    sig = jax.nn.sigmoid(pre)
    rest = 1.0 - sig
    slope = sig * (1.0 + pre * rest)
    bend = sig * rest * (2.0 + pre * (1.0 - 2.0 * sig))
    third = lin * bend * tangent
    return (lin * slope, slope * tangent, third, third * tangent)


def body(tokens, cotangent, expert_route, w_gate, w_up, w_down, sign_seeds):
    expert_count = lax.axis_size(EXPERT)
    ys, cores = lax.axis_size("y"), lax.axis_size("c")
    y, core = lax.axis_index("y"), lax.axis_index("c")
    tok_count, model_width = tokens.shape
    hidden_cols = w_gate.shape[2]
    slot_count = max(2, 2 * tok_count // expert_count)
    rows = expert_count * slot_count
    width = model_width // (ys * cores)
    barrier = lax.optimization_barrier

    def to_experts(send):
        return exchange(send.reshape(expert_count, slot_count, -1)).reshape(rows, -1)

    def neighbours(piece):
        return [shift_y(piece, -1), shift_y(piece, 1)]

    def both_cores(own):
        return jnp.concatenate([own, swap_cores(own)], axis=0)

    dispatch, send = dispatch_rows(expert_route, tokens, cotangent, rows, width)
    received, seed = barrier((to_experts(send), sign_seeds))
    mats, down = stage_weights(seed, w_gate, w_up, w_down)
    piece = received.T
    near = neighbours(piece)
    crossed = swap_cores(piece)
    near, mats, down, crossed = barrier((near, mats, down, crossed))
    x_far = shift_y(near[0][:width], -1)
    cot_far = shift_y(near[1][width:], 1)
    joint = jnp.concatenate(near, axis=0)
    other = swap_cores(joint)
    near = near + [piece, other[: 2 * width], other[2 * width :], crossed]
    x_near = [part[:width] for part in near]
    cot_near = [part[width:] for part in near]
    split = 2 * width
    sums = dot(mats[split:], jnp.concatenate(x_near, axis=0), 0, 0)
    sums, cot_near, x_far = barrier((sums, cot_near, x_far))
    x_far = both_cores(x_far)
    cot_sum = dot(down[:, split:], jnp.concatenate(cot_near, axis=0), 1, 0)
    sums, x_far, cot_sum, cot_far = barrier((sums, x_far, cot_sum, cot_far))
    cot_far = both_cores(cot_far)
    spans = [slice(at * hidden_cols, (at + 1) * hidden_cols) for at in range(3)]
    factors = forward_factors(*[sums[span] + dot(mats[:split, span], x_far, 0, 0) for span in spans])
    factors, cot_far = barrier((factors, cot_far))
    h = cot_sum + dot(down[:, :split], cot_far, 1, 0)
    curvature = jnp.sum(h * factors[3], axis=1)
    grads = jnp.concatenate([(h * f).astype(BF16) for f in (factors[2], factors[1], factors[0])], axis=0)

    def partial(start, count):
        return dot(mats[start * width : (start + count) * width], grads, 1, 0)

    give_far = partial(1, 1).astype(BF16)
    give_far, grads = barrier((give_far, grads))
    give_rest = partial(5, 3).astype(BF16)
    swapped = swap_cores(give_far)
    swapped, give_rest, grads = barrier((swapped, give_rest, grads))
    sum_far = partial(0, 1) + swapped.astype(F32)
    sum_far, grads = barrier((sum_far, grads))
    sum_rest = partial(2, 3) + swap_cores(give_rest).astype(F32)
    total = sum_rest[2 * width :] + shift_y(sum_far.astype(BF16), 2).astype(F32)
    for at, shift in enumerate((1, 3)):
        total = total + shift_y(sum_rest[at * width : (at + 1) * width].astype(BF16), shift).astype(F32)
    returned = to_experts(total.astype(BF16).T)
    combined = dot(dispatch, returned, 0, 0).astype(BF16)
    steps = (2, 1, 3, 0)
    own = jnp.stack([shift_y(combined, ys - step) for step in steps[:-1]] + [combined])
    result = jnp.zeros((tok_count, model_width), BF16)
    for blocks, of_core in ((own, core), (swap_cores(own), 1 - core)):
        for at, step in enumerate(steps):
            column = (of_core * ys + lax.rem(y + step, ys)) * width
            result = lax.dynamic_update_slice_in_dim(result, blocks[at], column, 1)
    return (result, curvature[None, :])


def solution(mesh):
    chips = Mesh(mesh.devices.reshape(4, 8, 4, 2), ("x", "z", "y", "c"))
    expert, dp = EXPERT, ("y", "c")
    in_specs = (
        P(expert, None),
        P(expert, None),
        P(expert, None),
        P(expert, None, dp),
        P(expert, None, dp),
        P(expert, dp, None),
        P(expert),
    )
    out_specs = (P(expert, None), P(expert, dp))
    return jax.shard_map(body, mesh=chips, in_specs=in_specs, out_specs=out_specs, check_vma=False)
```

```python
import functools
import math

import jax
import jax.numpy as jnp
from jax import lax
from jax.experimental import pallas as pl
from jax.experimental.pallas import tpu as pltpu
from jax.sharding import Mesh, PartitionSpec as P

EXPERT = ("x", "z")
SWAP = [(0, 1), (1, 0)]
BF16 = jnp.bfloat16
F32 = jnp.float32
VMEM = 63 * 1024 * 1024


BLOCKS = ((0, 2), (1, 2), (0, 1), (0, 3), (0, 0), (1, 1), (1, 3), (1, 0))


def dispatch_kernel(route_hbm, tokens_ref, cot_ref, dispatch_ref, send_ref, route_ref, pieces, sems):
    count = route_hbm.shape[1]
    slots, width = dispatch_ref.shape[0], send_ref.shape[1] // 2
    slot_count = slots // lax.axis_size(EXPERT)
    start = (lax.axis_index("c") * lax.axis_size("y") + lax.axis_index("y")) * width
    columns = pl.ds(pl.multiple_of(start, width), width)
    copies = [
        pltpu.make_async_copy(ref.at[:, columns], pieces.at[:, pl.ds(at * width, width)], sems.at[at])
        for at, ref in enumerate((tokens_ref, cot_ref))
    ]
    copies.append(pltpu.make_async_copy(route_hbm, route_ref, sems.at[2]))
    for copy in reversed(copies):
        copy.start()
    copies.pop().wait()
    across = jnp.broadcast_to(route_ref[...], (count, count))
    down = across.T
    earlier = (down == across) & (
        lax.broadcasted_iota(jnp.int32, (count, count), 0) < lax.broadcasted_iota(jnp.int32, (count, count), 1)
    )
    place = jnp.sum(jnp.where(earlier, 1.0, 0.0), axis=0, keepdims=True).astype(jnp.int32)
    target = route_ref[...] * slot_count + place
    slot = lax.broadcasted_iota(jnp.int32, (slots, count), 0)
    dispatch = jnp.where(slot == target, 1.0, 0.0).astype(BF16)
    dispatch_ref[...] = dispatch
    for copy in copies:
        copy.wait()
    send_ref[...] = jnp.dot(dispatch, pieces[...], preferred_element_type=F32).astype(BF16)


def dispatch_rows(route, tokens, cotangent, slots, width):
    count = tokens.shape[0]
    vmem = pl.BlockSpec(memory_space=pltpu.VMEM)
    hbm = pl.BlockSpec(memory_space=pltpu.HBM)
    return pl.pallas_call(
        dispatch_kernel,
        out_shape=[jax.ShapeDtypeStruct((slots, count), BF16), pltpu.VMEM((slots, 2 * width), BF16)],
        in_specs=[hbm, hbm, hbm],
        out_specs=[vmem, vmem],
        scratch_shapes=[
            pltpu.VMEM((1, count), jnp.int32),
            pltpu.VMEM((count, 2 * width), BF16),
            pltpu.SemaphoreType.DMA((3,)),
        ],
        compiler_params=pltpu.CompilerParams(vmem_limit_bytes=24 * 1024 * 1024),
        name="dispatch",
    )(*[pltpu.with_memory_space_constraint(a, pltpu.HBM) for a in (route.reshape(1, count), tokens, cotangent)])


def stage_kernel(seed_ref, gate_ref, up_ref, down_ref, mats_ref, cuts_ref, sems):
    hidden = gate_ref.shape[2]
    ys = lax.axis_size("y")
    y, core = lax.axis_index("y"), lax.axis_index("c")
    width = mats_ref.shape[0] // len(BLOCKS)

    def block(other, step):
        return lax.rem(core + other, 2) * ys + lax.rem(y + step, ys)

    copies = []
    for at, (other, step) in enumerate(BLOCKS):
        source = pl.ds(pl.multiple_of(block(other, step) * width, width), width)
        target = pl.ds(at * width, width)
        for which, (from_ref, to_ref) in enumerate(
            (
                (gate_ref.at[0, source, :], mats_ref.at[target, pl.ds(0, hidden)]),
                (up_ref.at[0, source, :], mats_ref.at[target, pl.ds(hidden, hidden)]),
                (down_ref.at[0, :, source], cuts_ref.at[:, target]),
            )
        ):
            copies.append(pltpu.make_async_copy(from_ref, to_ref, sems.at[3 * at + which]))
    for copy in copies:
        copy.start()

    offset = (y * lax.axis_size("c") + core) * hidden
    col = lax.broadcasted_iota(jnp.int32, (1, hidden), 1) + offset
    base = col * jnp.int32(19349663) + seed_ref[0] * jnp.int32(83492791)
    scale = jnp.asarray(1.0 / math.sqrt(2048), BF16).astype(F32)
    count = 16

    def signs(at, first, step):
        row = lax.broadcasted_iota(jnp.int32, (count, 1), 0) + (first * width + step * count)
        mixed = row * jnp.int32(73856093) + base
        mixed = mixed ^ mixed >> 15
        mixed = mixed * jnp.int32(735632791)
        mixed = mixed ^ mixed >> 13
        mixed = mixed * jnp.int32(1274126177)
        mixed = mixed ^ mixed >> 16
        target = pl.ds(pl.multiple_of(at * width + step * count, count), count)
        mats_ref[target, 2 * hidden :] = jnp.where((mixed & 32) != 0, scale, -scale).astype(BF16)

    for at, (other, step) in enumerate(BLOCKS):
        first = block(other, step)
        lax.fori_loop(0, width // count, lambda i, _: signs(at, first, i), None, unroll=4)
    for copy in copies:
        copy.wait()


def stage_weights(seed, w_gate, w_up, w_down):
    model, hidden = w_gate.shape[1:]
    vmem = pl.BlockSpec(memory_space=pltpu.VMEM)
    hbm = pl.BlockSpec(memory_space=pltpu.HBM)
    return pl.pallas_call(
        stage_kernel,
        out_shape=[jax.ShapeDtypeStruct((model, 3 * hidden), BF16), jax.ShapeDtypeStruct((hidden, model), BF16)],
        in_specs=[pl.BlockSpec(memory_space=pltpu.SMEM), hbm, hbm, hbm],
        out_specs=[vmem, vmem],
        scratch_shapes=[pltpu.SemaphoreType.DMA((3 * len(BLOCKS),))],
        compiler_params=pltpu.CompilerParams(vmem_limit_bytes=24 * 1024 * 1024),
        cost_estimate=pl.CostEstimate(flops=0, bytes_accessed=14 * model * hidden, transcendentals=0),
        name="stage_weights",
    )(seed, *[pltpu.with_memory_space_constraint(w, pltpu.HBM) for w in (w_gate, w_up, w_down)])


def dot(a, b, ca, cb):
    return lax.dot_general(a, b, (((ca,), (cb,)), ((), ())), preferred_element_type=F32)


def shift_y(value, shift):
    count = lax.axis_size("y")
    return lax.ppermute(value, "y", [(i, (i + shift) % count) for i in range(count)])


def swap_cores(value):
    return lax.ppermute(value, "c", SWAP)


def exchange(value):
    return lax.all_to_all(value, EXPERT, split_axis=0, concat_axis=0, tiled=True)


def forward_factors(pre, lin, tangent):
    sig = jax.nn.sigmoid(pre)
    rest = 1.0 - sig
    slope = sig * (1.0 + pre * rest)
    bend = sig * rest * (2.0 + pre * (1.0 - 2.0 * sig))
    third = lin * bend * tangent
    return (lin * slope, slope * tangent, third, third * tangent)


def body(tokens, cotangent, expert_route, w_gate, w_up, w_down, sign_seeds):
    expert_count = lax.axis_size(EXPERT)
    ys, cores = lax.axis_size("y"), lax.axis_size("c")
    y, core = lax.axis_index("y"), lax.axis_index("c")
    tok_count, model_width = tokens.shape
    hidden_cols = w_gate.shape[2]
    slot_count = max(2, 2 * tok_count // expert_count)
    rows = expert_count * slot_count
    width = model_width // (ys * cores)
    barrier = lax.optimization_barrier

    def to_experts(send):
        return exchange(send.reshape(expert_count, slot_count, -1)).reshape(rows, -1)

    def neighbours(piece):
        return [shift_y(piece, -1), shift_y(piece, 1)]

    def both_cores(own):
        return jnp.concatenate([own, swap_cores(own)], axis=0)

    dispatch, send = dispatch_rows(expert_route, tokens, cotangent, rows, width)
    received, seed = barrier((to_experts(send), sign_seeds))
    mats, down = stage_weights(seed, w_gate, w_up, w_down)
    piece = received.T
    near = neighbours(piece)
    crossed = swap_cores(piece)
    near, mats, down, crossed = barrier((near, mats, down, crossed))
    x_far = shift_y(near[0][:width], -1)
    cot_far = shift_y(near[1][width:], 1)
    joint = jnp.concatenate(near, axis=0)
    other = swap_cores(joint)
    near = near + [piece, other[: 2 * width], other[2 * width :], crossed]
    x_near = [part[:width] for part in near]
    cot_near = [part[width:] for part in near]
    split = 2 * width
    sums = dot(mats[split:], jnp.concatenate(x_near, axis=0), 0, 0)
    sums, cot_near, x_far = barrier((sums, cot_near, x_far))
    x_far = both_cores(x_far)
    cot_sum = dot(down[:, split:], jnp.concatenate(cot_near, axis=0), 1, 0)
    sums, x_far, cot_sum, cot_far = barrier((sums, x_far, cot_sum, cot_far))
    cot_far = both_cores(cot_far)
    spans = [slice(at * hidden_cols, (at + 1) * hidden_cols) for at in range(3)]
    factors = forward_factors(*[sums[span] + dot(mats[:split, span], x_far, 0, 0) for span in spans])
    factors, cot_far = barrier((factors, cot_far))
    h = cot_sum + dot(down[:, :split], cot_far, 1, 0)
    curvature = jnp.sum(h * factors[3], axis=1)
    grads = jnp.concatenate([(h * f).astype(BF16) for f in (factors[2], factors[1], factors[0])], axis=0)

    def partial(start, count):
        return dot(mats[start * width : (start + count) * width], grads, 1, 0)

    give_far = partial(1, 1).astype(BF16)
    give_far, grads = barrier((give_far, grads))
    give_rest = partial(5, 3).astype(BF16)
    swapped = swap_cores(give_far)
    swapped, give_rest, grads = barrier((swapped, give_rest, grads))
    sum_far = partial(0, 1) + swapped.astype(F32)
    sum_far, grads = barrier((sum_far, grads))
    sum_rest = partial(2, 3) + swap_cores(give_rest).astype(F32)
    total = sum_rest[2 * width :] + shift_y(sum_far.astype(BF16), 2).astype(F32)
    for at, shift in enumerate((1, 3)):
        total = total + shift_y(sum_rest[at * width : (at + 1) * width].astype(BF16), shift).astype(F32)
    returned = to_experts(total.astype(BF16).T)
    combined = dot(dispatch, returned, 0, 0).astype(BF16)
    steps = (2, 1, 3, 0)
    own = jnp.stack([shift_y(combined, ys - step) for step in steps[:-1]] + [combined])
    result = jnp.zeros((tok_count, model_width), BF16)
    for blocks, of_core in ((own, core), (swap_cores(own), 1 - core)):
        for at, step in enumerate(steps):
            column = (of_core * ys + lax.rem(y + step, ys)) * width
            result = lax.dynamic_update_slice_in_dim(result, blocks[at], column, 1)
    return (result, curvature[None, :])


def solution(mesh):
    chips = Mesh(mesh.devices.reshape(4, 8, 4, 2), ("x", "z", "y", "c"))
    expert, dp = EXPERT, ("y", "c")
    in_specs = (
        P(expert, None),
        P(expert, None),
        P(expert, None),
        P(expert, None, dp),
        P(expert, None, dp),
        P(expert, dp, None),
        P(expert),
    )
    out_specs = (P(expert, None), P(expert, dp))
    return jax.shard_map(body, mesh=chips, in_specs=in_specs, out_specs=out_specs, check_vma=False)
```
